512 devices in a mesh: energy: 64 (over z, y), slab: 8 (over x, core).
Axes of the slice: x: 4, y: 8, z: 8, core: 2. Of those that a mesh axis runs over, the one named last changes fastest.
Arguments:
- lesser_free: float32 [128, 144, 1024], P('energy', None, 'slab'), may hold values from -6 to 6
- greater_free: float32 [128, 144, 1024], P('energy', None, 'slab'), may hold values from -6 to 6
- retarded: float32 [128, 144, 1024], P('energy', None, 'slab'), may hold values from -1.75 to 1.75
- coupling: float32 [12, 144, 1024], P(None, None, 'slab'), may hold values from -0.875 to 0.875
- neighbour_offsets: int32 [12, 1024], P(None, 'slab'), may hold values from -32 to 32, as said below
- phonon_shift: int32 [64], replicated, may hold values from 1 to 16, as said below
- phonon_coupling: float32 [64], replicated, may hold values from 0.01 to 0.1
- phonon_occupation: float32 [64], replicated, may hold values from 0.05 to 5
Outputs:
- green_lesser: float32 [128, 144, 1024], P('energy', None, 'slab')
- green_greater: float32 [128, 144, 1024], P('energy', None, 'slab')
The draws below stay inside these ranges and needn't reach their ends.
Inputs may be any that keep to these rules, and one draw needn't show every extreme that they name: `neighbour_offsets`: each atom's 12 offsets are distinct and nonzero. `phonon_shift`: several frequencies may share a shift.
All inputs are finite; a program needn't handle non-finite values.
Results may differ from the reference program's by a relative error of at most 0.0003.
Values sent between devices are 32-bit elements; how exact they have to be, the bound alone decides.
A program may use at most 64 MiB of HBM per device.

```python
import math
import jax
import jax.numpy as jnp
from jax import lax

NORB = 12
NB = 12
NW = 64
SMAX = 16
HW = 32
ITERS = 2
NE = 128
ATOMS = 1024


def draw_neighbour_offsets(key, part):
    count = 2 * HW
    slots = jnp.arange(count, dtype=jnp.int32)
    candidates = jnp.where(slots < HW, slots - HW, slots - HW + 1)
    scores = jax.random.randint(key, (ATOMS, count), 0, 1 << 20, dtype=jnp.int32) * count + slots[None, :]
    atoms = jnp.arange(ATOMS, dtype=jnp.int32)
    boost = ((atoms[:, None] == 0) & ((slots[None, :] == 0) | (slots[None, :] == count - 1))).astype(jnp.int32) * (1 << 28)
    selected_pick = lax.top_k(scores + boost, NB)[1]
    return jnp.take(candidates, selected_pick).T.astype(jnp.int32)


def draw_phonon_shift(key, part):
    shifts = jax.random.randint(key, (NW,), 1, SMAX + 1, dtype=jnp.int32)
    first = jax.random.randint(jax.random.fold_in(key, 11), (), 0, NW, dtype=jnp.int32)
    second = (first + 1 + jax.random.randint(jax.random.fold_in(key, 12), (), 0, NW - 1, dtype=jnp.int32)) % NW
    slots = jnp.arange(NW, dtype=jnp.int32)
    shifts = jnp.where(slots == first, SMAX, shifts)
    return jnp.where(slots == second, 1, shifts).astype(jnp.int32)


def level_of(stream_key, dims, split, least, high):
    loudness, own = 1.0, jax.random.fold_in(stream_key, 6)
    for axis_at, shards_of in split:
        heights = jnp.exp(jax.random.uniform(jax.random.fold_in(own, axis_at), (shards_of,), jnp.float32, least / len(split), high / len(split)))
        loudness = loudness * jnp.repeat(heights, dims[axis_at] // shards_of).reshape([-1 if axis == axis_at else 1 for axis in range(len(dims))])
    return loudness


def centred(rng, dims, deviation, limit, split=(), kind=jnp.bfloat16):
    gain = level_of(rng, dims, split, -0.22, 0.18) if split else 1.0
    result = jax.random.normal(rng, dims, jnp.float32) * deviation * gain
    return jnp.minimum(jnp.maximum(result, -limit), limit).astype(kind)


def setup_inputs(seed: int = 0) -> dict:
    key_list = jax.random.split(jax.random.key(seed), 9)
    return {
        "lesser_free": centred(key_list[0], (NE, NORB * NORB, ATOMS), 1.0, 6.0, ((0, 64), (2, 8)), jnp.float32),
        "greater_free": centred(key_list[1], (NE, NORB * NORB, ATOMS), 1.0, 6.0, ((0, 64), (2, 8)), jnp.float32),
        "retarded": centred(key_list[2], (NE, NORB * NORB, ATOMS), NORB ** -0.5, 1.75, ((0, 64), (2, 8)), jnp.float32),
        "coupling": centred(key_list[3], (NB, NORB * NORB, ATOMS), (NORB * 4) ** -0.5, 0.875, ((2, 8),), jnp.float32),
        "neighbour_offsets": draw_neighbour_offsets(jax.random.fold_in(key_list[8], 71), 0),
        "phonon_shift": draw_phonon_shift(jax.random.fold_in(key_list[8], 71), 0),
        "phonon_coupling": jnp.clip(jnp.exp(jax.random.uniform(key_list[6], (NW,), jnp.float32, math.log(0.01), math.log(0.1))), 0.01, 0.1),
        "phonon_occupation": jnp.clip(jnp.exp(jax.random.uniform(key_list[7], (NW,), jnp.float32, math.log(0.05), math.log(5.0))), 0.05, 5.0),
    }


TOP_RANK = lax.Precision.HIGHEST


def mixing(upper_weight, downward_weight, shifts):
    places = jnp.arange(NE, dtype=jnp.int32)
    spacing = places[None, :] - places[:, None]

    def add_mode(kernel, mode):
        upper, lower, shift = mode
        kernel = kernel + upper * (spacing == shift).astype(jnp.float32) + lower * (spacing == -shift).astype(jnp.float32)
        return kernel, None

    kernel, _ = lax.scan(add_mode, jnp.zeros((NE, NE), jnp.float32), (upper_weight, downward_weight, shifts))
    return kernel


def couple(green, links, energy_displacements):
    padded = jnp.pad(green, ((0, 0), (0, 0), (0, 0), (HW, HW)))
    atoms = jnp.arange(ATOMS, dtype=jnp.int32)

    def add_neighbour(total, neighbour):
        link, offset = neighbour
        near = jnp.take(padded, atoms + offset + HW, axis=3)
        inner = jnp.einsum('ija,ejla->eila', link, near, precision=TOP_RANK)
        return total + jnp.einsum('eila,kla->eika', inner, link, precision=TOP_RANK), None

    total, _ = lax.scan(add_neighbour, jnp.zeros(green.shape, jnp.float32), (links, energy_displacements))
    return total


def dress(retarded_blocks, sigma):
    inner = jnp.einsum('eija,ejla->eila', retarded_blocks, sigma, precision=TOP_RANK)
    return jnp.einsum('eila,ekla->eika', inner, retarded_blocks, precision=TOP_RANK)


def reference(lesser_free, greater_free, retarded, coupling, neighbour_offsets, phonon_shift, phonon_coupling, phonon_occupation):
    blocks = (NE, NORB, NORB, ATOMS)
    emit = phonon_coupling * (phonon_occupation + 1.0)
    absorb = phonon_coupling * phonon_occupation
    kernel_stack = (mixing(emit, absorb, phonon_shift), mixing(absorb, emit, phonon_shift))
    frees = (lesser_free.reshape(blocks), greater_free.reshape(blocks))
    retarded_blocks = retarded.reshape(blocks)
    links = coupling.reshape(NB, NORB, NORB, ATOMS)
    greens = frees
    for step in range(ITERS):
        updated = []
        for kernel, free, green in zip(kernel_stack, frees, greens):
            coupled = couple(green, links, neighbour_offsets)
            sigma = jnp.dot(kernel, coupled.reshape(NE, -1), precision=TOP_RANK).reshape(blocks)
            updated.append(free + dress(retarded_blocks, sigma))
        greens = tuple(updated)
    target = (NE, NORB * NORB, ATOMS)
    return greens[0].reshape(target), greens[1].reshape(target)
```

```python
import functools

import jax
import jax.numpy as jnp
from jax import lax
from jax.experimental import pallas as pl
from jax.experimental.pallas import tpu as pltpu
from jax.sharding import PartitionSpec as P

NORB = 12
NB = 12
ITERS = 2
RING = 8
PAIRS = NORB * NORB
ROWS = 2 * PAIRS
PIECE = 40
PADDED = RING * PIECE
LANES = 128
MESH = pl.DeviceIdType.MESH


def spread(row):
    return jnp.broadcast_to(row, (8, LANES))


def rows8(start):
    return pl.ds(start, 8)


def gather_row(own, halo, near, inside, index, v):
    a = jnp.take_along_axis(own[rows8(8 * v), :], index, axis=1, mode="promise_in_bounds")
    h = jnp.take_along_axis(halo[rows8(8 * v), :], index, axis=1, mode="promise_in_bounds")
    near[v] = jnp.where(inside, a, h)


def gather_index(offsets, n):
    place = lax.broadcasted_iota(jnp.int32, (8, LANES), 1) + spread(offsets[pl.ds(n, 1), :])
    inside = (place >= 0) & (place < LANES)
    return inside, place & (LANES - 1)


def sandwich_step(n, links, wide_links, near, total, fetch):
    inner = [[None] * 3 for _ in range(NORB)]
    for j in range(NORB):
        block = [near[3 * j + l] for l in range(3)]
        for l in range(3):
            fetch(3 * j + l)
        for i in range(NORB):
            factor = spread(links[n, pl.ds(i * NORB + j, 1), :])
            for l in range(3):
                term = factor * block[l]
                inner[i][l] = term if j == 0 else inner[i][l] + term
    for k in range(NORB):
        start = n * ROWS
        right = [wide_links[rows8(pl.multiple_of(start + 8 * (3 * k + l), 8)), :] for l in range(3)]
        for i in range(NORB):
            term = inner[i][0] * right[0] + inner[i][1] * right[1] + inner[i][2] * right[2]
            total[i * NORB + k] += term


def fold(parts):
    sub = lax.broadcasted_iota(jnp.int32, (8, LANES), 0)
    low = sub < 4
    even = (sub & 2) == 0

    def halves(a, b):
        return jnp.where(low, a, b) + pltpu.roll(jnp.where(low, b, a), 4, 0)

    first = halves(parts[0], parts[2])
    second = halves(parts[1], parts[3])
    other = jnp.where(even, second, first)
    moved = jnp.where(even, pltpu.roll(first, 6, 0), pltpu.roll(second, 2, 0))
    del other
    return jnp.where(even, first, second) + moved


def dress(sigma, free, target, narrow, wide):
    inner = [[None] * 3 for _ in range(NORB)]
    for j in range(NORB):
        block = [sigma[rows8(8 * (3 * j + l)), :] for l in range(3)]
        for i in range(NORB):
            factor = narrow[i * NORB + j]
            for l in range(3):
                term = factor * block[l]
                inner[i][l] = term if j == 0 else inner[i][l] + term
    for i in range(NORB):
        for k3 in range(3):
            parts = []
            for q in range(4):
                k = 4 * k3 + q
                right = [wide[rows8(8 * (3 * k + l)), :] for l in range(3)]
                parts.append(inner[i][0] * right[0] + inner[i][1] * right[1] + inner[i][2] * right[2])
            at = 8 * (3 * i + k3)
            target[rows8(at), :] = free[rows8(at), :] + fold(parts)


def hop(m):
    half = (m + 1) // 2
    return 4 + half * (2 * (m % 2) - 1)


def kernel(
    lesser, greater, retarded, coupling, offsets, shifts, strength, occupation,
    out_lesser, out_greater,
    free_in, ret_in, links, wide_links, narrow_ret, wide_ret, taps, even_taps, odd_taps,
    lesser_buf, greater_buf, coupled, arrived, mixed, band, left_in, right_in,
    near_a, near_b, halo, total, sigma,
    load_sem, a1_send, a1_recv, z_send, z_recv, a2_send, a2_recv, x_send, x_recv,
):
    energy = lax.axis_index("energy")
    slab = lax.axis_index("slab")
    z = energy // RING
    y = energy % RING
    slabs = lax.axis_size("slab")
    planes = lax.axis_size("energy") // RING
    above = ((z + 1) % planes) * RING + y
    below = ((z + planes - 1) % planes) * RING + y
    right = (slab + 1) % slabs
    left = (slab + slabs - 1) % slabs

    loads = [
        pltpu.make_async_copy(lesser, free_in.at[0], load_sem.at[0]),
        pltpu.make_async_copy(greater, free_in.at[1], load_sem.at[1]),
        pltpu.make_async_copy(retarded, ret_in, load_sem.at[2]),
        pltpu.make_async_copy(coupling, links, load_sem.at[3]),
    ]
    for load in loads:
        load.start()

    barrier = pltpu.get_barrier_semaphore()

    def greet(m, carry):
        pl.semaphore_signal(
            barrier, inc=1, device_id=(z * RING + (y + hop(m)) % RING, slab), device_id_type=MESH
        )
        return carry

    lax.fori_loop(0, RING - 1, greet, 0)
    for peer in ((above, slab), (below, slab), (energy, right), (energy, left)):
        pl.semaphore_signal(barrier, inc=1, device_id=peer, device_id_type=MESH)

    def source(kind, t):
        return lesser_buf.at[t] if kind == 0 else coupled.at[t]

    def remote(src, dst, send, recv, peer):
        return pltpu.make_async_remote_copy(
            src_ref=src, dst_ref=dst, send_sem=send, recv_sem=recv, device_id=peer, device_id_type=MESH
        )

    def await_bytes(ref, sem):
        pltpu.make_async_copy(ref, ref, sem).wait()

    def piece(index):
        return pl.ds(pl.multiple_of(index * PIECE, 8), PIECE)

    def spread_start(kind, t):
        held = source(kind, t)

        def send(m, carry):
            to = (y + hop(m)) % RING
            remote(
                held.at[piece(to)], band.at[kind, t, piece(RING + y)],
                a1_send.at[kind, t, m], a1_recv.at[kind, t, m], (z * RING + to, slab),
            ).start()
            return carry

        pltpu.make_async_copy(
            held.at[piece(y)], band.at[kind, t, piece(RING + y)], a1_recv.at[kind, t, RING - 1]
        ).start()
        lax.fori_loop(0, RING - 1, send, 0)

    def spread_forward(kind, t):
        def pass_on(s, carry):
            m = (s + RING - 1) % RING
            origin = (y + RING - hop(m) * (1 - m // (RING - 1))) % RING
            here = band.at[kind, t, piece(RING + origin)]
            await_bytes(here, a1_recv.at[kind, t, m])
            remote(
                here, band.at[kind, t, piece(origin)],
                z_send.at[kind, t, 0, m], z_recv.at[kind, t, 0, m], (above, slab),
            ).start()
            remote(
                here, band.at[kind, t, piece(2 * RING + origin)],
                z_send.at[kind, t, 1, m], z_recv.at[kind, t, 1, m], (below, slab),
            ).start()
            return carry

        lax.fori_loop(0, RING, pass_on, 0)

    def mix(kind, t):
        def arrive(m, carry):
            for side in range(2):
                await_bytes(band.at[kind, t, piece(0)], z_recv.at[kind, t, side, m])
            return carry

        lax.fori_loop(0, RING, arrive, 0)

        @pl.when(z == 0)
        def _():
            band[kind, t, pl.ds(0, PADDED), :] = jnp.zeros((PADDED, LANES), jnp.float32)

        @pl.when(z == planes - 1)
        def _():
            band[kind, t, pl.ds(2 * PADDED, PADDED), :] = jnp.zeros((PADDED, LANES), jnp.float32)

        odd = (lax.broadcasted_iota(jnp.int32, (8, LANES), 0) & 1) == 1

        def blend(m, carry):
            to = (y + hop(m) * (1 - m // (RING - 1))) % RING
            tiles = PIECE // 8
            same = [None] * tiles
            swap = [None] * tiles
            for d in range(2 * RING + 1):
                first = odd_taps[kind, d]
                second = even_taps[kind, d]
                for r in range(tiles):
                    value = band[kind, t, rows8(pl.multiple_of((to + d) * PIECE + 8 * r, 8)), :]
                    term = value * first
                    swap[r] = term if d == 0 else swap[r] + term
                    if d != RING:
                        term = value * second
                        same[r] = term if d == 0 else same[r] + term
            for r in range(tiles):
                other = jnp.where(odd, pltpu.roll(swap[r], 1, 0), pltpu.roll(swap[r], 7, 0))
                mixed[kind, t, rows8(pl.multiple_of(m * PIECE + 8 * r, 8)), :] = same[r] + other

            @pl.when(m < RING - 1)
            def _():
                remote(
                    mixed.at[kind, t, piece(m)], arrived.at[kind, t, piece(y)],
                    a2_send.at[kind, t, m], a2_recv.at[kind, t, m], (z * RING + to, slab),
                ).start()

            @pl.when(m == RING - 1)
            def _():
                pltpu.make_async_copy(
                    mixed.at[kind, t, piece(m)], arrived.at[kind, t, piece(y)], a2_recv.at[kind, t, m]
                ).start()

            return carry

        lax.fori_loop(0, RING, blend, 0)

    def collect(kind, t, forward):
        def take(m, carry):
            origin = (y + RING - hop(m) * (1 - m // (RING - 1))) % RING
            here = arrived.at[kind, t, piece(origin)]
            await_bytes(here, a2_recv.at[kind, t, m])
            if forward:
                remote(
                    here, left_in.at[kind, t, piece(origin)],
                    x_send.at[kind, t, 0, m], x_recv.at[kind, t, 0, m], (energy, right),
                ).start()
                remote(
                    here, right_in.at[kind, t, piece(origin)],
                    x_send.at[kind, t, 1, m], x_recv.at[kind, t, 1, m], (energy, left),
                ).start()
            return carry

        lax.fori_loop(0, RING, take, 0)

    def edges_start(t):
        here = greater_buf.at[t]
        remote(here, left_in.at[1, t], x_send.at[1, t, 0, 0], x_recv.at[1, t, 0, 0], (energy, right)).start()
        remote(here, right_in.at[1, t], x_send.at[1, t, 1, 0], x_recv.at[1, t, 1, 0], (energy, left)).start()

    lane = lax.broadcasted_iota(jnp.int32, (8, LANES), 1)
    low_lanes = lane < LANES // 2
    edge_ok = jnp.where(low_lanes, slabs - 1 - slab, slab) > 0

    def edges_finish(kind, t):
        if kind == 1:
            await_bytes(left_in.at[1, t], x_recv.at[1, t, 0, 0])
            await_bytes(right_in.at[1, t], x_recv.at[1, t, 1, 0])
        else:
            def arrive(m, carry):
                for side in range(2):
                    await_bytes(left_in.at[0, t, piece(0)], x_recv.at[0, t, side, m])
                return carry

            lax.fori_loop(0, RING, arrive, 0)
        for v in range(ROWS // 8):
            value = jnp.where(low_lanes, right_in[kind, t, rows8(8 * v), :], left_in[kind, t, rows8(8 * v), :])
            halo[rows8(8 * v), :] = jnp.where(edge_ok, value, 0.0)

    def couple_first(own):
        inside, index = gather_index(offsets, 0)
        for v in range(ROWS // 8):
            gather_row(own, halo, near_a, inside, index, v)
        total[...] = jnp.zeros(total.shape, jnp.float32)

    def couple_part(own, begin, end):
        def step(h, carry):
            n = 2 * h
            inside, index = gather_index(offsets, n + 1)
            sandwich_step(
                n, links, wide_links, near_a, total,
                lambda v: gather_row(own, halo, near_b, inside, index, v),
            )
            inside_b, index_b = gather_index(offsets, (n + 2) % NB)
            sandwich_step(
                n + 1, links, wide_links, near_b, total,
                lambda v: gather_row(own, halo, near_a, inside_b, index_b, v),
            )
            return carry

        lax.fori_loop(begin, end, step, 0)

    def couple_last(target):
        for i in range(NORB):
            for k3 in range(3):
                target[rows8(8 * (3 * i + k3)), :] = fold([total[i * NORB + 4 * k3 + q] for q in range(4)])

    def interleave(kind, target):
        for e in range(2):
            for v in range(PAIRS // 8):
                target[pl.ds(16 * v + e, 8, stride=2), :] = free_in[kind, e, rows8(8 * v), :]

    zeros = jnp.zeros((PADDED - ROWS, LANES), jnp.float32)

    loads[0].wait()
    interleave(0, lesser_buf.at[0])
    for t in range(ITERS):
        lesser_buf[t, pl.ds(ROWS, PADDED - ROWS), :] = zeros
        greater_buf[t, pl.ds(ROWS, PADDED - ROWS), :] = zeros
        coupled[t, pl.ds(ROWS, PADDED - ROWS), :] = zeros
    pl.semaphore_wait(barrier, RING + 3)
    spread_start(0, 0)
    loads[1].wait()
    interleave(1, greater_buf.at[0])
    edges_start(0)

    row = lax.broadcasted_iota(jnp.int32, (PIECE, shifts.shape[1]), 0) - 17
    up = row == shifts[...]
    down = row == -shifts[...]
    emit = strength[...] * (occupation[...] + 1.0)
    absorb = strength[...] * occupation[...]
    for kind, (high, low) in enumerate(((emit, absorb), (absorb, emit))):
        column = jnp.sum(jnp.where(up, high, 0.0) + jnp.where(down, low, 0.0), axis=1, keepdims=True)
        taps[kind] = jnp.broadcast_to(column, (PIECE, LANES))
    odd_row = (lax.broadcasted_iota(jnp.int32, (8, LANES), 0) & 1) == 1
    for kind in range(2):
        for d in range(2 * RING + 1):
            even_taps[kind, d] = spread(taps[kind, pl.ds(2 * d + 1, 1), :])
            odd_taps[kind, d] = jnp.where(
                odd_row, spread(taps[kind, pl.ds(2 * d + 2, 1), :]), spread(taps[kind, pl.ds(2 * d, 1), :])
            )

    loads[2].wait()
    for r in range(PAIRS):
        narrow_ret[r] = jnp.where(odd_row, spread(ret_in[1, pl.ds(r, 1), :]), spread(ret_in[0, pl.ds(r, 1), :]))
    for e in range(2):
        for v in range(PAIRS // 8):
            wide_ret[pl.ds(16 * v + e, 8, stride=2), :] = ret_in[e, rows8(8 * v), :]
    loads[3].wait()

    def widen(n, carry):
        for v in range(PAIRS // 8):
            value = links[n, rows8(8 * v), :]
            for e in range(2):
                wide_links[pl.ds(n * ROWS + 16 * v + e, 8, stride=2), :] = value
        return carry

    lax.fori_loop(0, NB, widen, 0)

    def iteration(t, carry):
        spread_forward(0, t)
        edges_finish(1, t)
        own = greater_buf.at[t]
        couple_first(own)
        couple_part(own, 0, 3)
        mix(0, t)
        couple_part(own, 3, 6)
        couple_last(coupled.at[t])
        spread_start(1, t)
        collect(0, t, True)
        spread_forward(1, t)
        edges_finish(0, t)
        own = arrived.at[0, t]
        couple_first(own)
        couple_part(own, 0, 3)
        mix(1, t)
        couple_part(own, 3, 6)
        couple_last(sigma)
        dress(sigma, lesser_buf.at[0], lesser_buf.at[t + 1], narrow_ret, wide_ret)

        @pl.when(t < ITERS - 1)
        def _():
            spread_start(0, t + 1)

        collect(1, t, False)
        dress(arrived.at[1, t], greater_buf.at[0], greater_buf.at[t + 1], narrow_ret, wide_ret)

        @pl.when(t < ITERS - 1)
        def _():
            edges_start(t + 1)

        return carry

    lax.fori_loop(0, ITERS, iteration, 0)

    for e in range(2):
        for v in range(PAIRS // 8):
            out_lesser[e, rows8(8 * v), :] = lesser_buf[ITERS, pl.ds(16 * v + e, 8, stride=2), :]
            out_greater[e, rows8(8 * v), :] = greater_buf[ITERS, pl.ds(16 * v + e, 8, stride=2), :]

    def drain(t, carry):
        def pieces(m, inner):
            for kind in range(2):
                here = band.at[kind, t, piece(RING)]
                for side in range(2):
                    await_bytes(here, z_send.at[kind, t, side, m])

            for side in range(2):
                await_bytes(arrived.at[0, t, piece(0)], x_send.at[0, t, side, m])
            return inner

        def sent(m, inner):
            for kind in range(2):
                await_bytes(band.at[kind, t, piece(RING)], a1_send.at[kind, t, m])
                await_bytes(mixed.at[kind, t, piece(0)], a2_send.at[kind, t, m])
            return inner

        lax.fori_loop(0, RING, pieces, 0)
        lax.fori_loop(0, RING - 1, sent, 0)
        for side in range(2):
            await_bytes(greater_buf.at[t], x_send.at[1, t, side, 0])
        return carry

    lax.fori_loop(0, ITERS, drain, 0)


def body(lesser, greater, retarded, coupling, offsets, shifts, strength, occupation):
    f32 = jnp.float32
    vmem = functools.partial(pl.BlockSpec, memory_space=pltpu.VMEM)
    anywhere = functools.partial(pl.BlockSpec, memory_space=pl.ANY)
    lanes = lesser.shape[-1]
    dma = pltpu.SemaphoreType.DMA
    return pl.pallas_call(
        kernel,
        out_shape=(jax.ShapeDtypeStruct(lesser.shape, f32),) * 2,
        in_specs=[anywhere()] * 4 + [vmem()] * 4,
        out_specs=(vmem(), vmem()),
        scratch_shapes=[
            pltpu.VMEM((2, 2, PAIRS, lanes), f32),
            pltpu.VMEM((2, PAIRS, lanes), f32),
            pltpu.VMEM((NB, PAIRS, lanes), f32),
            pltpu.VMEM((NB * ROWS, lanes), f32),
            pltpu.VMEM((PAIRS, 8, lanes), f32),
            pltpu.VMEM((ROWS, lanes), f32),
            pltpu.VMEM((2, PIECE, lanes), f32),
            pltpu.VMEM((2, 2 * RING + 1, 8, lanes), f32),
            pltpu.VMEM((2, 2 * RING + 1, 8, lanes), f32),
            pltpu.VMEM((ITERS + 1, PADDED, lanes), f32),
            pltpu.VMEM((ITERS + 1, PADDED, lanes), f32),
            pltpu.VMEM((ITERS, PADDED, lanes), f32),
            pltpu.VMEM((2, ITERS, PADDED, lanes), f32),
            pltpu.VMEM((2, ITERS, PADDED, lanes), f32),
            pltpu.VMEM((2, ITERS, 3 * PADDED, lanes), f32),
            pltpu.VMEM((2, ITERS, PADDED, lanes), f32),
            pltpu.VMEM((2, ITERS, PADDED, lanes), f32),
            pltpu.VMEM((ROWS // 8, 8, lanes), f32),
            pltpu.VMEM((ROWS // 8, 8, lanes), f32),
            pltpu.VMEM((ROWS, lanes), f32),
            pltpu.VMEM((PAIRS, 8, lanes), f32),
            pltpu.VMEM((ROWS, lanes), f32),
            dma((4,)),
            dma((2, ITERS, RING - 1)),
            dma((2, ITERS, RING)),
            dma((2, ITERS, 2, RING)),
            dma((2, ITERS, 2, RING)),
            dma((2, ITERS, RING - 1)),
            dma((2, ITERS, RING)),
            dma((2, ITERS, 2, RING)),
            dma((2, ITERS, 2, RING)),
        ],
        compiler_params=pltpu.CompilerParams(
            collective_id=0, has_side_effects=True, vmem_limit_bytes=40 * 1024 * 1024
        ),
    )(
        lesser, greater, retarded, coupling, offsets,
        shifts.reshape(1, -1), strength.reshape(1, -1), occupation.reshape(1, -1),
    )


def solution(mesh):
    placed = (
        P("energy", None, "slab"),
        P("energy", None, "slab"),
        P("energy", None, "slab"),
        P(None, None, "slab"),
        P(None, "slab"),
        P(),
        P(),
        P(),
    )
    return jax.shard_map(
        body,
        mesh=mesh,
        in_specs=placed,
        out_specs=(P("energy", None, "slab"), P("energy", None, "slab")),
        check_vma=False,
    )
```

```python
import functools

import jax
import jax.numpy as jnp
from jax import lax
from jax.experimental import pallas as pl
from jax.experimental.pallas import tpu as pltpu
from jax.sharding import PartitionSpec as P

NORB = 12
NB = 12
ITERS = 2
RING = 8
PAIRS = NORB * NORB
ROWS = 2 * PAIRS
PIECE = 40
PADDED = RING * PIECE
LANES = 128
MESH = pl.DeviceIdType.MESH


def spread(row):
    return jnp.broadcast_to(row, (8, LANES))


def rows8(start):
    return pl.ds(start, 8)


def pick(source, v, index):
    return jnp.take_along_axis(source[rows8(8 * v), :], index, axis=1, mode="promise_in_bounds")


def sandwich_step(n, links, wide_links, near, total):
    inner = [[None] * 3 for _ in range(NORB)]
    for j in range(NORB):
        block = [near[n, 3 * j + l] for l in range(3)]
        for i in range(NORB):
            factor = spread(links[n, pl.ds(i * NORB + j, 1), :])
            for l in range(3):
                term = factor * block[l]
                inner[i][l] = term if j == 0 else inner[i][l] + term
    for k in range(NORB):
        start = n * ROWS
        right = [wide_links[rows8(pl.multiple_of(start + 8 * (3 * k + l), 8)), :] for l in range(3)]
        for i in range(NORB):
            term = inner[i][0] * right[0] + inner[i][1] * right[1] + inner[i][2] * right[2]
            total[i * NORB + k] += term


def fold(parts):
    sub = lax.broadcasted_iota(jnp.int32, (8, LANES), 0)
    low = sub < 4
    even = (sub & 2) == 0

    def halves(a, b):
        return jnp.where(low, a, b) + pltpu.roll(jnp.where(low, b, a), 4, 0)

    first = halves(parts[0], parts[2])
    second = halves(parts[1], parts[3])
    other = jnp.where(even, second, first)
    moved = jnp.where(even, pltpu.roll(first, 6, 0), pltpu.roll(second, 2, 0))
    del other
    return jnp.where(even, first, second) + moved


def dress(sigma, free, target, narrow, wide):
    inner = [[None] * 3 for _ in range(NORB)]
    for j in range(NORB):
        block = [sigma[rows8(8 * (3 * j + l)), :] for l in range(3)]
        for i in range(NORB):
            factor = narrow[i * NORB + j]
            for l in range(3):
                term = factor * block[l]
                inner[i][l] = term if j == 0 else inner[i][l] + term
    for i in range(NORB):
        for k3 in range(3):
            parts = []
            for q in range(4):
                k = 4 * k3 + q
                right = [wide[rows8(8 * (3 * k + l)), :] for l in range(3)]
                parts.append(inner[i][0] * right[0] + inner[i][1] * right[1] + inner[i][2] * right[2])
            at = 8 * (3 * i + k3)
            target[rows8(at), :] = free[rows8(at), :] + fold(parts)


def hop(m):
    half = (m + 1) // 2
    return 4 + half * (2 * (m % 2) - 1)


def kernel(
    lesser, greater, retarded, coupling, offsets_in, shifts_in, strength_in, occupation_in,
    out_lesser, out_greater,
    offsets, shifts, strength, occupation, free_in, ret_in, links, wide_links, narrow_ret, wide_ret, taps, even_taps, odd_taps,
    lesser_buf, greater_buf, coupled, arrived, mixed, band, left_in, right_in,
    pair_links, wide_pairs, stash, halo, total, sigma,
    load_sem, a1_send, a1_recv, z_send, z_recv, a2_send, a2_recv, x_send, x_recv,
):
    energy = lax.axis_index("energy")
    slab = lax.axis_index("slab")
    z = energy // RING
    y = energy % RING
    slabs = lax.axis_size("slab")
    planes = lax.axis_size("energy") // RING
    above = ((z + 1) % planes) * RING + y
    below = ((z + planes - 1) % planes) * RING + y
    right = (slab + 1) % slabs
    left = (slab + slabs - 1) % slabs

    loads = [
        pltpu.make_async_copy(lesser, free_in.at[0], load_sem.at[0]),
        pltpu.make_async_copy(greater, free_in.at[1], load_sem.at[1]),
        pltpu.make_async_copy(retarded, ret_in, load_sem.at[2]),
        pltpu.make_async_copy(coupling, links, load_sem.at[3]),
        pltpu.make_async_copy(offsets_in, offsets, load_sem.at[4]),
        pltpu.make_async_copy(shifts_in, shifts, load_sem.at[5]),
        pltpu.make_async_copy(strength_in, strength, load_sem.at[6]),
        pltpu.make_async_copy(occupation_in, occupation, load_sem.at[7]),
    ]
    barrier = pltpu.get_barrier_semaphore()

    def greet(m, carry):
        pl.semaphore_signal(
            barrier, inc=1, device_id=(z * RING + (y + hop(m)) % RING, slab), device_id_type=MESH
        )
        return carry

    lax.fori_loop(0, RING - 1, greet, 0)
    for peer in ((above, slab), (below, slab), (energy, right), (energy, left)):
        pl.semaphore_signal(barrier, inc=1, device_id=peer, device_id_type=MESH)
    for load in loads:
        load.start()

    def source(kind, t):
        return lesser_buf.at[t] if kind == 0 else coupled.at[t]

    def remote(src, dst, send, recv, peer):
        return pltpu.make_async_remote_copy(
            src_ref=src, dst_ref=dst, send_sem=send, recv_sem=recv, device_id=peer, device_id_type=MESH
        )

    def await_bytes(ref, sem):
        pltpu.make_async_copy(ref, ref, sem).wait()

    def piece(index):
        return pl.ds(pl.multiple_of(index * PIECE, 8), PIECE)

    def spread_start(kind, t):
        held = source(kind, t)

        def send(m, carry):
            to = (y + hop(m)) % RING
            remote(
                held.at[piece(to)], band.at[kind, t, piece(RING + y)],
                a1_send.at[kind, t, m], a1_recv.at[kind, t, m], (z * RING + to, slab),
            ).start()
            return carry

        pltpu.make_async_copy(
            held.at[piece(y)], band.at[kind, t, piece(RING + y)], a1_recv.at[kind, t, RING - 1]
        ).start()
        lax.fori_loop(0, RING - 1, send, 0)
        pass_on(kind, t, RING - 1, y)

    def pass_on(kind, t, m, origin):
        here = band.at[kind, t, piece(RING + origin)]
        await_bytes(here, a1_recv.at[kind, t, m])
        remote(
            here, band.at[kind, t, piece(origin)],
            z_send.at[kind, t, 0, m], z_recv.at[kind, t, 0, m], (above, slab),
        ).start()
        remote(
            here, band.at[kind, t, piece(2 * RING + origin)],
            z_send.at[kind, t, 1, m], z_recv.at[kind, t, 1, m], (below, slab),
        ).start()

    def pass_near(kind, t, m):
        pass_on(kind, t, m, (y + RING - hop(m)) % RING)

    def spread_forward(kind, t):
        def one(m, carry):
            pass_near(kind, t, m)
            return carry

        lax.fori_loop(0, RING - 1, one, 0)

    def mix(kind, t):
        def arrive(m, carry):
            for side in range(2):
                await_bytes(band.at[kind, t, piece(0)], z_recv.at[kind, t, side, m])
            return carry

        lax.fori_loop(0, RING, arrive, 0)

        @pl.when(z == 0)
        def _():
            band[kind, t, pl.ds(0, PADDED), :] = jnp.zeros((PADDED, LANES), jnp.float32)

        @pl.when(z == planes - 1)
        def _():
            band[kind, t, pl.ds(2 * PADDED, PADDED), :] = jnp.zeros((PADDED, LANES), jnp.float32)

        odd = (lax.broadcasted_iota(jnp.int32, (8, LANES), 0) & 1) == 1

        def blend(m, carry):
            to = (y + hop(m) * (1 - m // (RING - 1))) % RING
            tiles = PIECE // 8
            same = [None] * tiles
            swap = [None] * tiles
            for d in range(2 * RING + 1):
                first = odd_taps[kind, d]
                second = even_taps[kind, d]
                for r in range(tiles):
                    value = band[kind, t, rows8(pl.multiple_of((to + d) * PIECE + 8 * r, 8)), :]
                    term = value * first
                    swap[r] = term if d == 0 else swap[r] + term
                    if d != RING:
                        term = value * second
                        same[r] = term if d == 0 else same[r] + term
            for r in range(tiles):
                other = jnp.where(odd, pltpu.roll(swap[r], 1, 0), pltpu.roll(swap[r], 7, 0))
                mixed[kind, t, rows8(pl.multiple_of(m * PIECE + 8 * r, 8)), :] = same[r] + other

            @pl.when(m < RING - 1)
            def _():
                remote(
                    mixed.at[kind, t, piece(m)], arrived.at[kind, t, piece(y)],
                    a2_send.at[kind, t, m], a2_recv.at[kind, t, m], (z * RING + to, slab),
                ).start()

            @pl.when(m == RING - 1)
            def _():
                pltpu.make_async_copy(
                    mixed.at[kind, t, piece(m)], arrived.at[kind, t, piece(y)], a2_recv.at[kind, t, m]
                ).start()

            return carry

        lax.fori_loop(0, RING, blend, 0)

    def collect(kind, t, forward):
        def take(m, carry):
            origin = (y + RING - hop(m) * (1 - m // (RING - 1))) % RING
            here = arrived.at[kind, t, piece(origin)]
            await_bytes(here, a2_recv.at[kind, t, m])
            if forward:
                remote(
                    here, left_in.at[kind, t, piece(origin)],
                    x_send.at[kind, t, 0, m], x_recv.at[kind, t, 0, m], (energy, right),
                ).start()
                remote(
                    here, right_in.at[kind, t, piece(origin)],
                    x_send.at[kind, t, 1, m], x_recv.at[kind, t, 1, m], (energy, left),
                ).start()
            return carry

        lax.fori_loop(0, RING, take, 0)

    def edges_start(t):
        here = greater_buf.at[t]
        remote(here, left_in.at[1, t], x_send.at[1, t, 0, 0], x_recv.at[1, t, 0, 0], (energy, right)).start()
        remote(here, right_in.at[1, t], x_send.at[1, t, 1, 0], x_recv.at[1, t, 1, 0], (energy, left)).start()

    lane = lax.broadcasted_iota(jnp.int32, (8, LANES), 1)
    low_lanes = lane < LANES // 2
    edge_ok = jnp.where(low_lanes, slabs - 1 - slab, slab) > 0
    outer = (lane < LANES // 4) | (lane >= LANES - LANES // 4)

    def half_turn(value):
        return pltpu.roll(value, LANES // 2, 1)

    def edges_finish(kind, t):
        if kind == 1:
            await_bytes(left_in.at[1, t], x_recv.at[1, t, 0, 0])
            await_bytes(right_in.at[1, t], x_recv.at[1, t, 1, 0])
        else:
            def arrive(m, carry):
                for side in range(2):
                    await_bytes(left_in.at[0, t, piece(0)], x_recv.at[0, t, side, m])
                return carry

            lax.fori_loop(0, RING, arrive, 0)
        for v in range(ROWS // 8):
            value = jnp.where(low_lanes, right_in[kind, t, rows8(8 * v), :], left_in[kind, t, rows8(8 * v), :])
            value = jnp.where(edge_ok, value, 0.0)
            halo[rows8(8 * v), :] = jnp.where(outer, value, half_turn(value))

    def couple_own(own):
        def one(n, carry):
            place = lane + spread(offsets[pl.ds(n, 1), :])
            inside = (place >= 0) & (place < LANES)
            index = place & (LANES - 1)
            for v in range(ROWS // 8):
                stash[n, v] = jnp.where(inside, pick(own, v, index), 0.0)
            return carry

        lax.fori_loop(0, NB, one, 0)
        total[...] = jnp.zeros(total.shape, jnp.float32)

    def couple_steps(begin, end):
        def step(n, carry):
            sandwich_step(n, links, wide_links, stash, total)
            return carry

        lax.fori_loop(begin, end, step, 0)

    def folded(i, k3):
        return fold([total[i * NORB + 4 * k3 + q] for q in range(4)])

    def couple_inner(target):
        for i in range(NORB):
            for k3 in range(3):
                target[rows8(8 * (3 * i + k3)), :] = folded(i, k3)

    def couple_halo(target):
        def one(h, carry):
            near = spread(offsets[pl.ds(2 * h, 1), :])
            far = spread(offsets[pl.ds(2 * h + 1, 1), :])
            atom = jnp.where(outer, lane, lane ^ (LANES // 2))
            place = atom + jnp.where(outer, near, half_turn(far))
            beyond = (place < 0) | (place >= LANES)
            index = (place + jnp.where(outer, 0, LANES // 2)) & (LANES - 1)
            for v in range(ROWS // 8):
                stash[h, v] = jnp.where(beyond, pick(halo, v, index), 0.0)
            return carry

        lax.fori_loop(0, NB // 2, one, 0)
        total[...] = jnp.zeros(total.shape, jnp.float32)

        def step(h, carry):
            sandwich_step(h, pair_links, wide_pairs, stash, total)
            return carry

        lax.fori_loop(0, NB // 2, step, 0)
        for i in range(NORB):
            for k3 in range(3):
                at = rows8(8 * (3 * i + k3))
                value = folded(i, k3)
                target[at, :] += jnp.where(outer, value + half_turn(value), 0.0)

    def interleave(kind, target):
        for e in range(2):
            for v in range(PAIRS // 8):
                target[pl.ds(16 * v + e, 8, stride=2), :] = free_in[kind, e, rows8(8 * v), :]

    zeros = jnp.zeros((PADDED - ROWS, LANES), jnp.float32)

    loads[0].wait()
    interleave(0, lesser_buf.at[0])
    loads[1].wait()
    interleave(1, greater_buf.at[0])
    for t in range(ITERS):
        lesser_buf[t, pl.ds(ROWS, PADDED - ROWS), :] = zeros
        greater_buf[t, pl.ds(ROWS, PADDED - ROWS), :] = zeros
        coupled[t, pl.ds(ROWS, PADDED - ROWS), :] = zeros

    pl.semaphore_wait(barrier, RING + 3)
    spread_start(0, 0)
    edges_start(0)

    for load in loads[4:]:
        load.wait()
    row = lax.broadcasted_iota(jnp.int32, (PIECE, shifts.shape[1]), 0) - 17
    up = row == shifts[...]
    down = row == -shifts[...]
    emit = strength[...] * (occupation[...] + 1.0)
    absorb = strength[...] * occupation[...]
    for kind, (high, low) in enumerate(((emit, absorb), (absorb, emit))):
        column = jnp.sum(jnp.where(up, high, 0.0) + jnp.where(down, low, 0.0), axis=1, keepdims=True)
        taps[kind] = jnp.broadcast_to(column, (PIECE, LANES))
    odd_row = (lax.broadcasted_iota(jnp.int32, (8, LANES), 0) & 1) == 1
    for kind in range(2):
        for d in range(2 * RING + 1):
            even_taps[kind, d] = spread(taps[kind, pl.ds(2 * d + 1, 1), :])
            odd_taps[kind, d] = jnp.where(
                odd_row, spread(taps[kind, pl.ds(2 * d + 2, 1), :]), spread(taps[kind, pl.ds(2 * d, 1), :])
            )

    loads[2].wait()
    for r in range(PAIRS):
        narrow_ret[r] = jnp.where(odd_row, spread(ret_in[1, pl.ds(r, 1), :]), spread(ret_in[0, pl.ds(r, 1), :]))
    for e in range(2):
        for v in range(PAIRS // 8):
            wide_ret[pl.ds(16 * v + e, 8, stride=2), :] = ret_in[e, rows8(8 * v), :]
    loads[3].wait()

    def widen(n, carry):
        for v in range(PAIRS // 8):
            value = links[n, rows8(8 * v), :]
            for e in range(2):
                wide_links[pl.ds(n * ROWS + 16 * v + e, 8, stride=2), :] = value
        return carry

    lax.fori_loop(0, NB, widen, 0)

    def widen_pair(h, carry):
        for v in range(PAIRS // 8):
            value = jnp.where(outer, links[2 * h, rows8(8 * v), :], half_turn(links[2 * h + 1, rows8(8 * v), :]))
            pair_links[h, rows8(8 * v), :] = value
            for e in range(2):
                wide_pairs[pl.ds(h * ROWS + 16 * v + e, 8, stride=2), :] = value
        return carry

    lax.fori_loop(0, NB // 2, widen_pair, 0)
    couple_own(greater_buf.at[0])
    couple_steps(0, NB)
    couple_inner(coupled.at[0])

    def iteration(t, carry):
        spread_forward(0, t)
        edges_finish(1, t)
        couple_halo(coupled.at[t])
        spread_start(1, t)
        mix(0, t)
        spread_forward(1, t)
        collect(0, t, True)
        couple_own(arrived.at[0, t])
        couple_steps(0, NB // 2)
        mix(1, t)
        couple_steps(NB // 2, NB)
        couple_inner(sigma)
        edges_finish(0, t)
        couple_halo(sigma)
        dress(sigma, lesser_buf.at[0], lesser_buf.at[t + 1], narrow_ret, wide_ret)

        @pl.when(t < ITERS - 1)
        def _():
            spread_start(0, t + 1)

        collect(1, t, False)
        dress(arrived.at[1, t], greater_buf.at[0], greater_buf.at[t + 1], narrow_ret, wide_ret)

        @pl.when(t < ITERS - 1)
        def _():
            edges_start(t + 1)
            couple_own(greater_buf.at[t + 1])
            couple_steps(0, NB)
            couple_inner(coupled.at[t + 1])

        return carry

    lax.fori_loop(0, ITERS, iteration, 0)

    for e in range(2):
        for v in range(PAIRS // 8):
            out_lesser[e, rows8(8 * v), :] = lesser_buf[ITERS, pl.ds(16 * v + e, 8, stride=2), :]
            out_greater[e, rows8(8 * v), :] = greater_buf[ITERS, pl.ds(16 * v + e, 8, stride=2), :]

    def drain(t, carry):
        def pieces(m, inner):
            for kind in range(2):
                here = band.at[kind, t, piece(RING)]
                for side in range(2):
                    await_bytes(here, z_send.at[kind, t, side, m])

            for side in range(2):
                await_bytes(arrived.at[0, t, piece(0)], x_send.at[0, t, side, m])
            return inner

        def sent(m, inner):
            for kind in range(2):
                await_bytes(band.at[kind, t, piece(RING)], a1_send.at[kind, t, m])
                await_bytes(mixed.at[kind, t, piece(0)], a2_send.at[kind, t, m])
            return inner

        lax.fori_loop(0, RING, pieces, 0)
        lax.fori_loop(0, RING - 1, sent, 0)
        for side in range(2):
            await_bytes(greater_buf.at[t], x_send.at[1, t, side, 0])
        return carry

    lax.fori_loop(0, ITERS, drain, 0)


def body(lesser, greater, retarded, coupling, offsets, shifts, strength, occupation):
    f32 = jnp.float32
    vmem = functools.partial(pl.BlockSpec, memory_space=pltpu.VMEM)
    outside = functools.partial(pl.BlockSpec, memory_space=pltpu.HBM)
    lanes = lesser.shape[-1]
    dma = pltpu.SemaphoreType.DMA
    return pl.pallas_call(
        kernel,
        out_shape=(jax.ShapeDtypeStruct(lesser.shape, f32),) * 2,
        in_specs=[outside()] * 8,
        out_specs=(vmem(), vmem()),
        scratch_shapes=[
            pltpu.VMEM(offsets.shape, jnp.int32),
            pltpu.VMEM((1, shifts.shape[0]), jnp.int32),
            pltpu.VMEM((1, shifts.shape[0]), f32),
            pltpu.VMEM((1, shifts.shape[0]), f32),
            pltpu.VMEM((2, 2, PAIRS, lanes), f32),
            pltpu.VMEM((2, PAIRS, lanes), f32),
            pltpu.VMEM((NB, PAIRS, lanes), f32),
            pltpu.VMEM((NB * ROWS, lanes), f32),
            pltpu.VMEM((PAIRS, 8, lanes), f32),
            pltpu.VMEM((ROWS, lanes), f32),
            pltpu.VMEM((2, PIECE, lanes), f32),
            pltpu.VMEM((2, 2 * RING + 1, 8, lanes), f32),
            pltpu.VMEM((2, 2 * RING + 1, 8, lanes), f32),
            pltpu.VMEM((ITERS + 1, PADDED, lanes), f32),
            pltpu.VMEM((ITERS + 1, PADDED, lanes), f32),
            pltpu.VMEM((ITERS, PADDED, lanes), f32),
            pltpu.VMEM((2, ITERS, PADDED, lanes), f32),
            pltpu.VMEM((2, ITERS, PADDED, lanes), f32),
            pltpu.VMEM((2, ITERS, 3 * PADDED, lanes), f32),
            pltpu.VMEM((2, ITERS, PADDED, lanes), f32),
            pltpu.VMEM((2, ITERS, PADDED, lanes), f32),
            pltpu.VMEM((NB // 2, PAIRS, lanes), f32),
            pltpu.VMEM((NB // 2 * ROWS, lanes), f32),
            pltpu.VMEM((NB, ROWS // 8, 8, lanes), f32),
            pltpu.VMEM((ROWS, lanes), f32),
            pltpu.VMEM((PAIRS, 8, lanes), f32),
            pltpu.VMEM((ROWS, lanes), f32),
            dma((8,)),
            dma((2, ITERS, RING - 1)),
            dma((2, ITERS, RING)),
            dma((2, ITERS, 2, RING)),
            dma((2, ITERS, 2, RING)),
            dma((2, ITERS, RING - 1)),
            dma((2, ITERS, RING)),
            dma((2, ITERS, 2, RING)),
            dma((2, ITERS, 2, RING)),
        ],
        compiler_params=pltpu.CompilerParams(
            collective_id=0, has_side_effects=True, vmem_limit_bytes=63 * 1024 * 1024
        ),
    )(
        lesser, greater, retarded, coupling, offsets,
        shifts.reshape(1, -1), strength.reshape(1, -1), occupation.reshape(1, -1),
    )


def solution(mesh):
    placed = (
        P("energy", None, "slab"),
        P("energy", None, "slab"),
        P("energy", None, "slab"),
        P(None, None, "slab"),
        P(None, "slab"),
        P(),
        P(),
        P(),
    )
    return jax.shard_map(
        body,
        mesh=mesh,
        in_specs=placed,
        out_specs=(P("energy", None, "slab"), P("energy", None, "slab")),
        check_vma=False,
    )
```

```python
import functools

import jax
import jax.numpy as jnp
from jax import lax
from jax.experimental import pallas as pl
from jax.experimental.pallas import tpu as pltpu
from jax.sharding import PartitionSpec as P

NORB = 12
NB = 12
ITERS = 2
RING = 8
PAIRS = NORB * NORB
ROWS = 2 * PAIRS
PIECE = 40
PADDED = RING * PIECE
LANES = 128
MESH = pl.DeviceIdType.MESH


def spread(row):
    return jnp.broadcast_to(row, (8, LANES))


def rows8(start):
    return pl.ds(start, 8)


def sandwich_step(n, links, wide_links, near, total):
    inner = [[None] * 3 for _ in range(NORB)]
    for j in range(NORB):
        block = [near[n, 3 * j + l] for l in range(3)]
        for i in range(NORB):
            factor = spread(links[n, pl.ds(i * NORB + j, 1), :])
            for l in range(3):
                term = factor * block[l]
                inner[i][l] = term if j == 0 else inner[i][l] + term
    for k in range(NORB):
        start = n * ROWS
        right = [wide_links[rows8(pl.multiple_of(start + 8 * (3 * k + l), 8)), :] for l in range(3)]
        for i in range(NORB):
            term = inner[i][0] * right[0] + inner[i][1] * right[1] + inner[i][2] * right[2]
            total[i * NORB + k] += term


def fold(parts):
    sub = lax.broadcasted_iota(jnp.int32, (8, LANES), 0)
    low = sub < 4
    even = (sub & 2) == 0

    def halves(a, b):
        return jnp.where(low, a, b) + pltpu.roll(jnp.where(low, b, a), 4, 0)

    first = halves(parts[0], parts[2])
    second = halves(parts[1], parts[3])
    other = jnp.where(even, second, first)
    moved = jnp.where(even, pltpu.roll(first, 6, 0), pltpu.roll(second, 2, 0))
    del other
    return jnp.where(even, first, second) + moved


def dress(sigma, free, target, narrow, wide):
    inner = [[None] * 3 for _ in range(NORB)]
    for j in range(NORB):
        block = [sigma[rows8(8 * (3 * j + l)), :] for l in range(3)]
        for i in range(NORB):
            factor = narrow[i * NORB + j]
            for l in range(3):
                term = factor * block[l]
                inner[i][l] = term if j == 0 else inner[i][l] + term
    for i in range(NORB):
        for k3 in range(3):
            parts = []
            for q in range(4):
                k = 4 * k3 + q
                right = [wide[rows8(8 * (3 * k + l)), :] for l in range(3)]
                parts.append(inner[i][0] * right[0] + inner[i][1] * right[1] + inner[i][2] * right[2])
            at = 8 * (3 * i + k3)
            target[rows8(at), :] = free[rows8(at), :] + fold(parts)


def hop(m):
    half = (m + 1) // 2
    return 4 + half * (2 * (m % 2) - 1)


def kernel(
    lesser, greater, retarded, coupling, offsets_in, shifts_in, strength_in, occupation_in,
    out_lesser, out_greater,
    offsets, shifts, strength, occupation, free_in, ret_in, links, wide_links, narrow_ret, wide_ret, taps, even_taps, odd_taps,
    lesser_buf, greater_buf, coupled, arrived, mixed, band, left_in, right_in,
    pair_links, wide_pairs, inner_hot, outer_hot, halves, stash, halo, total, sigma,
    load_sem, a1_send, a1_recv, z_send, z_recv, a2_send, a2_recv, x_send, x_recv,
):
    energy = lax.axis_index("energy")
    slab = lax.axis_index("slab")
    z = energy // RING
    y = energy % RING
    slabs = lax.axis_size("slab")
    planes = lax.axis_size("energy") // RING
    above = ((z + 1) % planes) * RING + y
    below = ((z + planes - 1) % planes) * RING + y
    right = (slab + 1) % slabs
    left = (slab + slabs - 1) % slabs

    loads = [
        pltpu.make_async_copy(lesser, free_in.at[0], load_sem.at[0]),
        pltpu.make_async_copy(greater, free_in.at[1], load_sem.at[1]),
        pltpu.make_async_copy(retarded, ret_in, load_sem.at[2]),
        pltpu.make_async_copy(coupling, links, load_sem.at[3]),
        pltpu.make_async_copy(offsets_in, offsets, load_sem.at[4]),
        pltpu.make_async_copy(shifts_in, shifts, load_sem.at[5]),
        pltpu.make_async_copy(strength_in, strength, load_sem.at[6]),
        pltpu.make_async_copy(occupation_in, occupation, load_sem.at[7]),
    ]
    barrier = pltpu.get_barrier_semaphore()

    def greet(m, carry):
        pl.semaphore_signal(
            barrier, inc=1, device_id=(z * RING + (y + hop(m)) % RING, slab), device_id_type=MESH
        )
        return carry

    lax.fori_loop(0, RING - 1, greet, 0)
    for peer in ((above, slab), (below, slab), (energy, right), (energy, left)):
        pl.semaphore_signal(barrier, inc=1, device_id=peer, device_id_type=MESH)
    for load in loads:
        load.start()

    def source(kind, t):
        return lesser_buf.at[t] if kind == 0 else coupled.at[t]

    def remote(src, dst, send, recv, peer):
        return pltpu.make_async_remote_copy(
            src_ref=src, dst_ref=dst, send_sem=send, recv_sem=recv, device_id=peer, device_id_type=MESH
        )

    def await_bytes(ref, sem):
        pltpu.make_async_copy(ref, ref, sem).wait()

    def piece(index):
        return pl.ds(pl.multiple_of(index * PIECE, 8), PIECE)

    def spread_start(kind, t):
        held = source(kind, t)

        def send(m, carry):
            to = (y + hop(m)) % RING
            remote(
                held.at[piece(to)], band.at[kind, t, piece(RING + y)],
                a1_send.at[kind, t, m], a1_recv.at[kind, t, m], (z * RING + to, slab),
            ).start()
            return carry

        pltpu.make_async_copy(
            held.at[piece(y)], band.at[kind, t, piece(RING + y)], a1_recv.at[kind, t, RING - 1]
        ).start()
        lax.fori_loop(0, RING - 1, send, 0)
        pass_on(kind, t, RING - 1, y)

    def pass_on(kind, t, m, origin):
        here = band.at[kind, t, piece(RING + origin)]
        await_bytes(here, a1_recv.at[kind, t, m])
        remote(
            here, band.at[kind, t, piece(origin)],
            z_send.at[kind, t, 0, m], z_recv.at[kind, t, 0, m], (above, slab),
        ).start()
        remote(
            here, band.at[kind, t, piece(2 * RING + origin)],
            z_send.at[kind, t, 1, m], z_recv.at[kind, t, 1, m], (below, slab),
        ).start()

    def pass_near(kind, t, m):
        pass_on(kind, t, m, (y + RING - hop(m)) % RING)

    def spread_forward(kind, t):
        def one(m, carry):
            pass_near(kind, t, m)
            return carry

        lax.fori_loop(0, RING - 1, one, 0)

    def mix(kind, t):
        def arrive(m, carry):
            for side in range(2):
                await_bytes(band.at[kind, t, piece(0)], z_recv.at[kind, t, side, m])
            return carry

        lax.fori_loop(0, RING, arrive, 0)

        @pl.when(z == 0)
        def _():
            band[kind, t, pl.ds(0, PADDED), :] = jnp.zeros((PADDED, LANES), jnp.float32)

        @pl.when(z == planes - 1)
        def _():
            band[kind, t, pl.ds(2 * PADDED, PADDED), :] = jnp.zeros((PADDED, LANES), jnp.float32)

        odd = (lax.broadcasted_iota(jnp.int32, (8, LANES), 0) & 1) == 1

        def blend(m, carry):
            to = (y + hop(m) * (1 - m // (RING - 1))) % RING
            tiles = PIECE // 8
            same = [None] * tiles
            swap = [None] * tiles
            for d in range(2 * RING + 1):
                first = odd_taps[kind, d]
                second = even_taps[kind, d]
                for r in range(tiles):
                    value = band[kind, t, rows8(pl.multiple_of((to + d) * PIECE + 8 * r, 8)), :]
                    term = value * first
                    swap[r] = term if d == 0 else swap[r] + term
                    if d != RING:
                        term = value * second
                        same[r] = term if d == 0 else same[r] + term
            for r in range(tiles):
                other = jnp.where(odd, pltpu.roll(swap[r], 1, 0), pltpu.roll(swap[r], 7, 0))
                mixed[kind, t, rows8(pl.multiple_of(m * PIECE + 8 * r, 8)), :] = same[r] + other

            @pl.when(m < RING - 1)
            def _():
                remote(
                    mixed.at[kind, t, piece(m)], arrived.at[kind, t, piece(y)],
                    a2_send.at[kind, t, m], a2_recv.at[kind, t, m], (z * RING + to, slab),
                ).start()

            @pl.when(m == RING - 1)
            def _():
                pltpu.make_async_copy(
                    mixed.at[kind, t, piece(m)], arrived.at[kind, t, piece(y)], a2_recv.at[kind, t, m]
                ).start()

            return carry

        lax.fori_loop(0, RING, blend, 0)

    def collect(kind, t, forward):
        def take(m, carry):
            origin = (y + RING - hop(m) * (1 - m // (RING - 1))) % RING
            here = arrived.at[kind, t, piece(origin)]
            await_bytes(here, a2_recv.at[kind, t, m])
            if forward:
                remote(
                    here, left_in.at[kind, t, piece(origin)],
                    x_send.at[kind, t, 0, m], x_recv.at[kind, t, 0, m], (energy, right),
                ).start()
                remote(
                    here, right_in.at[kind, t, piece(origin)],
                    x_send.at[kind, t, 1, m], x_recv.at[kind, t, 1, m], (energy, left),
                ).start()
            return carry

        lax.fori_loop(0, RING, take, 0)

    def edges_start(t):
        here = greater_buf.at[t]
        remote(here, left_in.at[1, t], x_send.at[1, t, 0, 0], x_recv.at[1, t, 0, 0], (energy, right)).start()
        remote(here, right_in.at[1, t], x_send.at[1, t, 1, 0], x_recv.at[1, t, 1, 0], (energy, left)).start()

    lane = lax.broadcasted_iota(jnp.int32, (8, LANES), 1)
    low_lanes = lane < LANES // 2
    edge_ok = jnp.where(low_lanes, slabs - 1 - slab, slab) > 0
    outer = (lane < LANES // 4) | (lane >= LANES - LANES // 4)

    def half_turn(value):
        return pltpu.roll(value, LANES // 2, 1)

    def edges_finish(kind, t):
        if kind == 1:
            await_bytes(left_in.at[1, t], x_recv.at[1, t, 0, 0])
            await_bytes(right_in.at[1, t], x_recv.at[1, t, 1, 0])
        else:
            def arrive(m, carry):
                for side in range(2):
                    await_bytes(left_in.at[0, t, piece(0)], x_recv.at[0, t, side, m])
                return carry

            lax.fori_loop(0, RING, arrive, 0)
        for v in range(ROWS // 8):
            value = jnp.where(low_lanes, right_in[kind, t, rows8(8 * v), :], left_in[kind, t, rows8(8 * v), :])
            value = jnp.where(edge_ok, value, 0.0)
            halo[rows8(8 * v), :] = jnp.where(outer, value, half_turn(value))

    def take_near(source, table, count):
        value = source[pl.ds(0, ROWS), :]
        high = value.astype(jnp.bfloat16)
        halves[:, :LANES] = high
        halves[:, LANES:] = (value - high.astype(jnp.float32)).astype(jnp.bfloat16)

        for p in range(count):
            found = jnp.dot(halves[...], table[p], preferred_element_type=jnp.float32)
            stash[2 * p] = found[:, :LANES].reshape(ROWS // 8, 8, LANES)
            stash[2 * p + 1] = found[:, LANES:].reshape(ROWS // 8, 8, LANES)

    def mark(table, p, part, place):
        wanted = jnp.concatenate([place] * (LANES // 8), axis=0)
        row = lax.broadcasted_iota(jnp.int32, (LANES, LANES), 0)
        hot = jnp.where(row == wanted, 1.0, 0.0).astype(jnp.bfloat16)
        for copy in range(2):
            table[p, copy * LANES : (copy + 1) * LANES, part * LANES : (part + 1) * LANES] = hot

    def mark_inner(p, carry):
        for part in range(2):
            mark(inner_hot, p, part, lane + spread(offsets[pl.ds(2 * p + part, 1), :]))
        return carry

    def mark_outer(p, carry):
        for part in range(2):
            near = spread(offsets[pl.ds(4 * p + 2 * part, 1), :])
            far = spread(offsets[pl.ds(4 * p + 2 * part + 1, 1), :])
            atom = jnp.where(outer, lane, lane ^ (LANES // 2))
            place = atom + jnp.where(outer, near, half_turn(far))
            beyond = (place < 0) | (place >= LANES)
            index = (place + jnp.where(outer, 0, LANES // 2)) & (LANES - 1)
            mark(outer_hot, p, part, jnp.where(beyond, index, -1))
        return carry

    def couple_own(own):
        take_near(own, inner_hot, NB // 2)
        total[...] = jnp.zeros(total.shape, jnp.float32)

    def couple_steps(begin, end):
        def step(n, carry):
            sandwich_step(n, links, wide_links, stash, total)
            return carry

        lax.fori_loop(begin, end, step, 0)

    def folded(i, k3):
        return fold([total[i * NORB + 4 * k3 + q] for q in range(4)])

    def couple_inner(target):
        for i in range(NORB):
            for k3 in range(3):
                target[rows8(8 * (3 * i + k3)), :] = folded(i, k3)

    def couple_halo(target):
        take_near(halo, outer_hot, NB // 4)
        total[...] = jnp.zeros(total.shape, jnp.float32)

        def step(h, carry):
            sandwich_step(h, pair_links, wide_pairs, stash, total)
            return carry

        lax.fori_loop(0, NB // 2, step, 0)
        for i in range(NORB):
            for k3 in range(3):
                at = rows8(8 * (3 * i + k3))
                value = folded(i, k3)
                target[at, :] += jnp.where(outer, value + half_turn(value), 0.0)

    def interleave(kind, target):
        for e in range(2):
            for v in range(PAIRS // 8):
                target[pl.ds(16 * v + e, 8, stride=2), :] = free_in[kind, e, rows8(8 * v), :]

    zeros = jnp.zeros((PADDED - ROWS, LANES), jnp.float32)

    loads[0].wait()
    interleave(0, lesser_buf.at[0])
    loads[1].wait()
    interleave(1, greater_buf.at[0])
    for t in range(ITERS):
        lesser_buf[t, pl.ds(ROWS, PADDED - ROWS), :] = zeros
        greater_buf[t, pl.ds(ROWS, PADDED - ROWS), :] = zeros
        coupled[t, pl.ds(ROWS, PADDED - ROWS), :] = zeros

    pl.semaphore_wait(barrier, RING + 3)
    spread_start(0, 0)
    edges_start(0)

    for load in loads[4:]:
        load.wait()
    row = lax.broadcasted_iota(jnp.int32, (PIECE, shifts.shape[1]), 0) - 17
    up = row == shifts[...]
    down = row == -shifts[...]
    emit = strength[...] * (occupation[...] + 1.0)
    absorb = strength[...] * occupation[...]
    for kind, (high, low) in enumerate(((emit, absorb), (absorb, emit))):
        column = jnp.sum(jnp.where(up, high, 0.0) + jnp.where(down, low, 0.0), axis=1, keepdims=True)
        taps[kind] = jnp.broadcast_to(column, (PIECE, LANES))
    odd_row = (lax.broadcasted_iota(jnp.int32, (8, LANES), 0) & 1) == 1
    for kind in range(2):
        for d in range(2 * RING + 1):
            even_taps[kind, d] = spread(taps[kind, pl.ds(2 * d + 1, 1), :])
            odd_taps[kind, d] = jnp.where(
                odd_row, spread(taps[kind, pl.ds(2 * d + 2, 1), :]), spread(taps[kind, pl.ds(2 * d, 1), :])
            )

    loads[2].wait()
    for r in range(PAIRS):
        narrow_ret[r] = jnp.where(odd_row, spread(ret_in[1, pl.ds(r, 1), :]), spread(ret_in[0, pl.ds(r, 1), :]))
    for e in range(2):
        for v in range(PAIRS // 8):
            wide_ret[pl.ds(16 * v + e, 8, stride=2), :] = ret_in[e, rows8(8 * v), :]
    loads[3].wait()

    def widen(n, carry):
        for v in range(PAIRS // 8):
            value = links[n, rows8(8 * v), :]
            for e in range(2):
                wide_links[pl.ds(n * ROWS + 16 * v + e, 8, stride=2), :] = value
        return carry

    lax.fori_loop(0, NB, widen, 0)

    def widen_pair(h, carry):
        for v in range(PAIRS // 8):
            value = jnp.where(outer, links[2 * h, rows8(8 * v), :], half_turn(links[2 * h + 1, rows8(8 * v), :]))
            pair_links[h, rows8(8 * v), :] = value
            for e in range(2):
                wide_pairs[pl.ds(h * ROWS + 16 * v + e, 8, stride=2), :] = value
        return carry

    lax.fori_loop(0, NB // 2, widen_pair, 0)
    lax.fori_loop(0, NB // 2, mark_inner, 0)
    couple_own(greater_buf.at[0])
    couple_steps(0, NB)
    couple_inner(coupled.at[0])
    spread_forward(0, 0)
    lax.fori_loop(0, NB // 4, mark_outer, 0)

    def iteration(t, carry):
        edges_finish(1, t)
        couple_halo(coupled.at[t])
        spread_start(1, t)
        mix(0, t)
        spread_forward(1, t)
        collect(0, t, True)
        couple_own(arrived.at[0, t])
        couple_steps(0, NB // 4)
        mix(1, t)
        couple_steps(NB // 4, NB)
        couple_inner(sigma)
        edges_finish(0, t)
        couple_halo(sigma)
        dress(sigma, lesser_buf.at[0], lesser_buf.at[t + 1], narrow_ret, wide_ret)

        @pl.when(t < ITERS - 1)
        def _():
            spread_start(0, t + 1)

        collect(1, t, False)
        dress(arrived.at[1, t], greater_buf.at[0], greater_buf.at[t + 1], narrow_ret, wide_ret)

        @pl.when(t < ITERS - 1)
        def _():
            edges_start(t + 1)
            couple_own(greater_buf.at[t + 1])
            couple_steps(0, NB)
            couple_inner(coupled.at[t + 1])
            spread_forward(0, t + 1)

        return carry

    lax.fori_loop(0, ITERS, iteration, 0)

    for e in range(2):
        for v in range(PAIRS // 8):
            out_lesser[e, rows8(8 * v), :] = lesser_buf[ITERS, pl.ds(16 * v + e, 8, stride=2), :]
            out_greater[e, rows8(8 * v), :] = greater_buf[ITERS, pl.ds(16 * v + e, 8, stride=2), :]

    def drain(t, carry):
        def pieces(m, inner):
            for kind in range(2):
                here = band.at[kind, t, piece(RING)]
                for side in range(2):
                    await_bytes(here, z_send.at[kind, t, side, m])

            for side in range(2):
                await_bytes(arrived.at[0, t, piece(0)], x_send.at[0, t, side, m])
            return inner

        def sent(m, inner):
            for kind in range(2):
                await_bytes(band.at[kind, t, piece(RING)], a1_send.at[kind, t, m])
                await_bytes(mixed.at[kind, t, piece(0)], a2_send.at[kind, t, m])
            return inner

        lax.fori_loop(0, RING, pieces, 0)
        lax.fori_loop(0, RING - 1, sent, 0)
        for side in range(2):
            await_bytes(greater_buf.at[t], x_send.at[1, t, side, 0])
        return carry

    lax.fori_loop(0, ITERS, drain, 0)


def body(lesser, greater, retarded, coupling, offsets, shifts, strength, occupation):
    f32 = jnp.float32
    vmem = functools.partial(pl.BlockSpec, memory_space=pltpu.VMEM)
    outside = functools.partial(pl.BlockSpec, memory_space=pltpu.HBM)
    lanes = lesser.shape[-1]
    dma = pltpu.SemaphoreType.DMA
    return pl.pallas_call(
        kernel,
        out_shape=(jax.ShapeDtypeStruct(lesser.shape, f32),) * 2,
        in_specs=[outside()] * 8,
        out_specs=(vmem(), vmem()),
        scratch_shapes=[
            pltpu.VMEM(offsets.shape, jnp.int32),
            pltpu.VMEM((1, shifts.shape[0]), jnp.int32),
            pltpu.VMEM((1, shifts.shape[0]), f32),
            pltpu.VMEM((1, shifts.shape[0]), f32),
            pltpu.VMEM((2, 2, PAIRS, lanes), f32),
            pltpu.VMEM((2, PAIRS, lanes), f32),
            pltpu.VMEM((NB, PAIRS, lanes), f32),
            pltpu.VMEM((NB * ROWS, lanes), f32),
            pltpu.VMEM((PAIRS, 8, lanes), f32),
            pltpu.VMEM((ROWS, lanes), f32),
            pltpu.VMEM((2, PIECE, lanes), f32),
            pltpu.VMEM((2, 2 * RING + 1, 8, lanes), f32),
            pltpu.VMEM((2, 2 * RING + 1, 8, lanes), f32),
            pltpu.VMEM((ITERS + 1, PADDED, lanes), f32),
            pltpu.VMEM((ITERS + 1, PADDED, lanes), f32),
            pltpu.VMEM((ITERS, PADDED, lanes), f32),
            pltpu.VMEM((2, ITERS, PADDED, lanes), f32),
            pltpu.VMEM((2, ITERS, PADDED, lanes), f32),
            pltpu.VMEM((2, ITERS, 3 * PADDED, lanes), f32),
            pltpu.VMEM((2, ITERS, PADDED, lanes), f32),
            pltpu.VMEM((2, ITERS, PADDED, lanes), f32),
            pltpu.VMEM((NB // 2, PAIRS, lanes), f32),
            pltpu.VMEM((NB // 2 * ROWS, lanes), f32),
            pltpu.VMEM((NB // 2, 2 * lanes, 2 * lanes), jnp.bfloat16),
            pltpu.VMEM((NB // 4, 2 * lanes, 2 * lanes), jnp.bfloat16),
            pltpu.VMEM((ROWS, 2 * lanes), jnp.bfloat16),
            pltpu.VMEM((NB, ROWS // 8, 8, lanes), f32),
            pltpu.VMEM((ROWS, lanes), f32),
            pltpu.VMEM((PAIRS, 8, lanes), f32),
            pltpu.VMEM((ROWS, lanes), f32),
            dma((8,)),
            dma((2, ITERS, RING - 1)),
            dma((2, ITERS, RING)),
            dma((2, ITERS, 2, RING)),
            dma((2, ITERS, 2, RING)),
            dma((2, ITERS, RING - 1)),
            dma((2, ITERS, RING)),
            dma((2, ITERS, 2, RING)),
            dma((2, ITERS, 2, RING)),
        ],
        compiler_params=pltpu.CompilerParams(
            collective_id=0, has_side_effects=True, vmem_limit_bytes=63 * 1024 * 1024
        ),
    )(
        lesser, greater, retarded, coupling, offsets,
        shifts.reshape(1, -1), strength.reshape(1, -1), occupation.reshape(1, -1),
    )


def solution(mesh):
    placed = (
        P("energy", None, "slab"),
        P("energy", None, "slab"),
        P("energy", None, "slab"),
        P(None, None, "slab"),
        P(None, "slab"),
        P(),
        P(),
        P(),
    )
    return jax.shard_map(
        body,
        mesh=mesh,
        in_specs=placed,
        out_specs=(P("energy", None, "slab"), P("energy", None, "slab")),
        check_vma=False,
    )
```

```python
import functools

import jax
import jax.numpy as jnp
from jax import lax
from jax.experimental import pallas as pl
from jax.experimental.pallas import tpu as pltpu
from jax.sharding import PartitionSpec as P

NORB = 12
NB = 12
ITERS = 2
RING = 8
PAIRS = NORB * NORB
ROWS = 2 * PAIRS
PIECE = 40
PADDED = RING * PIECE
LANES = 128
MESH = pl.DeviceIdType.MESH


def spread(row):
    return jnp.broadcast_to(row, (8, LANES))


def rows8(start):
    return pl.ds(start, 8)


def sandwich_step(n, links, wide_links, near, total):
    inner = [[None] * 3 for _ in range(NORB)]
    for j in range(NORB):
        block = [near[n, 3 * j + l] for l in range(3)]
        for i in range(NORB):
            factor = spread(links[n, pl.ds(i * NORB + j, 1), :])
            for l in range(3):
                term = factor * block[l]
                inner[i][l] = term if j == 0 else inner[i][l] + term
    for k in range(NORB):
        start = n * ROWS
        right = [wide_links[rows8(pl.multiple_of(start + 8 * (3 * k + l), 8)), :] for l in range(3)]
        for i in range(NORB):
            term = inner[i][0] * right[0] + inner[i][1] * right[1] + inner[i][2] * right[2]
            total[i * NORB + k] += term


def fold(parts):
    sub = lax.broadcasted_iota(jnp.int32, (8, LANES), 0)
    low = sub < 4
    even = (sub & 2) == 0

    def halves(a, b):
        return jnp.where(low, a, b) + pltpu.roll(jnp.where(low, b, a), 4, 0)

    first = halves(parts[0], parts[2])
    second = halves(parts[1], parts[3])
    other = jnp.where(even, second, first)
    moved = jnp.where(even, pltpu.roll(first, 6, 0), pltpu.roll(second, 2, 0))
    del other
    return jnp.where(even, first, second) + moved


def dress(sigma, free, target, narrow, wide):
    inner = [[None] * 3 for _ in range(NORB)]
    for j in range(NORB):
        block = [sigma[rows8(8 * (3 * j + l)), :] for l in range(3)]
        for i in range(NORB):
            factor = narrow[i * NORB + j]
            for l in range(3):
                term = factor * block[l]
                inner[i][l] = term if j == 0 else inner[i][l] + term
    for i in range(NORB):
        for k3 in range(3):
            parts = []
            for q in range(4):
                k = 4 * k3 + q
                right = [wide[rows8(8 * (3 * k + l)), :] for l in range(3)]
                parts.append(inner[i][0] * right[0] + inner[i][1] * right[1] + inner[i][2] * right[2])
            at = 8 * (3 * i + k3)
            target[rows8(at), :] = free[rows8(at), :] + fold(parts)


def hop(m):
    half = (m + 1) // 2
    return 4 + half * (2 * (m % 2) - 1)


def kernel(
    lesser, greater, retarded, coupling, offsets_in, shifts_in, strength_in, occupation_in,
    out_lesser, out_greater,
    offsets, shifts, strength, occupation, free_in, ret_in, links, wide_links, narrow_ret, wide_ret, taps, even_taps, odd_taps,
    lesser_buf, greater_buf, coupled, arrived, mixed, band, left_in, right_in,
    pair_links, wide_pairs, inner_hot, outer_hot, halves, stash, halo, total, sigma,
    load_sem, a1_send, a1_recv, z_send, z_recv, a2_send, a2_recv, x_send, x_recv,
):
    energy = lax.axis_index("energy")
    slab = lax.axis_index("slab")
    z = energy // RING
    y = energy % RING
    slabs = lax.axis_size("slab")
    planes = lax.axis_size("energy") // RING
    above = ((z + 1) % planes) * RING + y
    below = ((z + planes - 1) % planes) * RING + y
    right = (slab + 1) % slabs
    left = (slab + slabs - 1) % slabs

    loads = [
        pltpu.make_async_copy(lesser, free_in.at[0], load_sem.at[0]),
        pltpu.make_async_copy(greater, free_in.at[1], load_sem.at[1]),
        pltpu.make_async_copy(retarded, ret_in, load_sem.at[2]),
        pltpu.make_async_copy(coupling, links, load_sem.at[3]),
        pltpu.make_async_copy(offsets_in, offsets, load_sem.at[4]),
        pltpu.make_async_copy(shifts_in, shifts, load_sem.at[5]),
        pltpu.make_async_copy(strength_in, strength, load_sem.at[6]),
        pltpu.make_async_copy(occupation_in, occupation, load_sem.at[7]),
    ]
    barrier = pltpu.get_barrier_semaphore()

    def greet(m, carry):
        pl.semaphore_signal(
            barrier, inc=1, device_id=(z * RING + (y + hop(m)) % RING, slab), device_id_type=MESH
        )
        return carry

    lax.fori_loop(0, RING - 1, greet, 0)
    for peer in ((above, slab), (below, slab), (energy, right), (energy, left)):
        pl.semaphore_signal(barrier, inc=1, device_id=peer, device_id_type=MESH)
    for load in loads:
        load.start()

    def source(kind, t):
        return lesser_buf.at[t] if kind == 0 else coupled.at[t]

    def remote(src, dst, send, recv, peer):
        return pltpu.make_async_remote_copy(
            src_ref=src, dst_ref=dst, send_sem=send, recv_sem=recv, device_id=peer, device_id_type=MESH
        )

    def await_bytes(ref, sem):
        pltpu.make_async_copy(ref, ref, sem).wait()

    def piece(index):
        return pl.ds(pl.multiple_of(index * PIECE, 8), PIECE)

    def spread_start(kind, t):
        held = source(kind, t)

        def send(m, carry):
            to = (y + hop(m)) % RING
            remote(
                held.at[piece(to)], band.at[kind, t, piece(RING + y)],
                a1_send.at[kind, t, m], a1_recv.at[kind, t, m], (z * RING + to, slab),
            ).start()
            return carry

        pltpu.make_async_copy(
            held.at[piece(y)], band.at[kind, t, piece(RING + y)], a1_recv.at[kind, t, RING - 1]
        ).start()
        lax.fori_loop(0, RING - 1, send, 0)
        pass_on(kind, t, RING - 1, y)

    def pass_on(kind, t, m, origin):
        here = band.at[kind, t, piece(RING + origin)]
        await_bytes(here, a1_recv.at[kind, t, m])
        remote(
            here, band.at[kind, t, piece(origin)],
            z_send.at[kind, t, 0, m], z_recv.at[kind, t, 0, m], (above, slab),
        ).start()
        remote(
            here, band.at[kind, t, piece(2 * RING + origin)],
            z_send.at[kind, t, 1, m], z_recv.at[kind, t, 1, m], (below, slab),
        ).start()

    def pass_near(kind, t, m):
        pass_on(kind, t, m, (y + RING - hop(m)) % RING)

    def spread_forward(kind, t):
        def one(m, carry):
            pass_near(kind, t, m)
            return carry

        lax.fori_loop(0, RING - 1, one, 0)

    def mix(kind, t):
        def arrive(m, carry):
            for side in range(2):
                await_bytes(band.at[kind, t, piece(0)], z_recv.at[kind, t, side, m])
            return carry

        lax.fori_loop(0, RING, arrive, 0)

        @pl.when(z == 0)
        def _():
            band[kind, t, pl.ds(0, PADDED), :] = jnp.zeros((PADDED, LANES), jnp.float32)

        @pl.when(z == planes - 1)
        def _():
            band[kind, t, pl.ds(2 * PADDED, PADDED), :] = jnp.zeros((PADDED, LANES), jnp.float32)

        odd = (lax.broadcasted_iota(jnp.int32, (8, LANES), 0) & 1) == 1

        def blend(m, carry):
            to = (y + hop(m) * (1 - m // (RING - 1))) % RING
            tiles = PIECE // 8
            same = [None] * tiles
            swap = [None] * tiles
            for d in range(2 * RING + 1):
                first = odd_taps[kind, d]
                second = even_taps[kind, d]
                for r in range(tiles):
                    value = band[kind, t, rows8(pl.multiple_of((to + d) * PIECE + 8 * r, 8)), :]
                    term = value * first
                    swap[r] = term if d == 0 else swap[r] + term
                    if d != RING:
                        term = value * second
                        same[r] = term if d == 0 else same[r] + term
            for r in range(tiles):
                other = jnp.where(odd, pltpu.roll(swap[r], 1, 0), pltpu.roll(swap[r], 7, 0))
                mixed[kind, t, rows8(pl.multiple_of(m * PIECE + 8 * r, 8)), :] = same[r] + other

            @pl.when(m < RING - 1)
            def _():
                remote(
                    mixed.at[kind, t, piece(m)], arrived.at[kind, t, piece(y)],
                    a2_send.at[kind, t, m], a2_recv.at[kind, t, m], (z * RING + to, slab),
                ).start()

            @pl.when(m == RING - 1)
            def _():
                pltpu.make_async_copy(
                    mixed.at[kind, t, piece(m)], arrived.at[kind, t, piece(y)], a2_recv.at[kind, t, m]
                ).start()

            return carry

        lax.fori_loop(0, RING, blend, 0)

    def collect(kind, t):
        def take(m, carry):
            origin = (y + RING - hop(m) * (1 - m // (RING - 1))) % RING
            here = arrived.at[kind, t, piece(origin)]
            await_bytes(here, a2_recv.at[kind, t, m])
            return carry

        lax.fori_loop(0, RING, take, 0)

    whole = pl.ds(0, ROWS)

    def edges_start(kind, held, t):
        here = held.at[whole]
        for side, (target, peer) in enumerate(((left_in, right), (right_in, left))):
            remote(
                here, target.at[kind, t, whole], x_send.at[kind, t, side], x_recv.at[kind, t, side], (energy, peer)
            ).start()

    lane = lax.broadcasted_iota(jnp.int32, (8, LANES), 1)
    low_lanes = lane < LANES // 2
    edge_ok = jnp.where(low_lanes, slabs - 1 - slab, slab) > 0
    outer = (lane < LANES // 4) | (lane >= LANES - LANES // 4)

    def half_turn(value):
        return pltpu.roll(value, LANES // 2, 1)

    def edges_finish(kind, t):
        for side, target in enumerate((left_in, right_in)):
            await_bytes(target.at[kind, t, whole], x_recv.at[kind, t, side])
        for v in range(ROWS // 8):
            value = jnp.where(low_lanes, right_in[kind, t, rows8(8 * v), :], left_in[kind, t, rows8(8 * v), :])
            value = jnp.where(edge_ok, value, 0.0)
            halo[rows8(8 * v), :] = jnp.where(outer, value, half_turn(value))

    def take_near(source, table, count):
        value = source[pl.ds(0, ROWS), :]
        high = value.astype(jnp.bfloat16)
        halves[:, :LANES] = high
        halves[:, LANES:] = (value - high.astype(jnp.float32)).astype(jnp.bfloat16)

        for p in range(count):
            found = jnp.dot(halves[...], table[p], preferred_element_type=jnp.float32)
            stash[2 * p] = found[:, :LANES].reshape(ROWS // 8, 8, LANES)
            stash[2 * p + 1] = found[:, LANES:].reshape(ROWS // 8, 8, LANES)

    def mark(table, p, part, place):
        wanted = jnp.concatenate([place] * (LANES // 8), axis=0)
        row = lax.broadcasted_iota(jnp.int32, (LANES, LANES), 0)
        hot = jnp.where(row == wanted, 1.0, 0.0).astype(jnp.bfloat16)
        for copy in range(2):
            table[p, copy * LANES : (copy + 1) * LANES, part * LANES : (part + 1) * LANES] = hot

    def mark_inner(p, carry):
        for part in range(2):
            mark(inner_hot, p, part, lane + spread(offsets[pl.ds(2 * p + part, 1), :]))
        return carry

    def mark_outer(p, carry):
        for part in range(2):
            near = spread(offsets[pl.ds(4 * p + 2 * part, 1), :])
            far = spread(offsets[pl.ds(4 * p + 2 * part + 1, 1), :])
            atom = jnp.where(outer, lane, lane ^ (LANES // 2))
            place = atom + jnp.where(outer, near, half_turn(far))
            beyond = (place < 0) | (place >= LANES)
            index = (place + jnp.where(outer, 0, LANES // 2)) & (LANES - 1)
            mark(outer_hot, p, part, jnp.where(beyond, index, -1))
        return carry

    def couple_own(own):
        take_near(own, inner_hot, NB // 2)
        total[...] = jnp.zeros(total.shape, jnp.float32)

    def couple_steps(begin, end):
        def step(n, carry):
            sandwich_step(n, links, wide_links, stash, total)
            return carry

        lax.fori_loop(begin, end, step, 0)

    def folded(i, k3):
        return fold([total[i * NORB + 4 * k3 + q] for q in range(4)])

    def couple_inner(target):
        for i in range(NORB):
            for k3 in range(3):
                target[rows8(8 * (3 * i + k3)), :] = folded(i, k3)

    def couple_halo(target):
        take_near(halo, outer_hot, NB // 4)
        total[...] = jnp.zeros(total.shape, jnp.float32)

        def step(h, carry):
            sandwich_step(h, pair_links, wide_pairs, stash, total)
            return carry

        lax.fori_loop(0, NB // 2, step, 0)
        for i in range(NORB):
            for k3 in range(3):
                at = rows8(8 * (3 * i + k3))
                value = folded(i, k3)
                target[at, :] += jnp.where(outer, value + half_turn(value), 0.0)

    def interleave(kind, target):
        for e in range(2):
            for v in range(PAIRS // 8):
                target[pl.ds(16 * v + e, 8, stride=2), :] = free_in[kind, e, rows8(8 * v), :]

    zeros = jnp.zeros((PADDED - ROWS, LANES), jnp.float32)

    loads[0].wait()
    interleave(0, lesser_buf.at[0])
    loads[1].wait()
    interleave(1, greater_buf.at[0])
    for t in range(ITERS):
        lesser_buf[t, pl.ds(ROWS, PADDED - ROWS), :] = zeros
        greater_buf[t, pl.ds(ROWS, PADDED - ROWS), :] = zeros
        coupled[t, pl.ds(ROWS, PADDED - ROWS), :] = zeros

    pl.semaphore_wait(barrier, RING + 3)
    spread_start(0, 0)
    edges_start(1, greater_buf.at[0], 0)

    for load in loads[4:]:
        load.wait()
    row = lax.broadcasted_iota(jnp.int32, (PIECE, shifts.shape[1]), 0) - 17
    up = row == shifts[...]
    down = row == -shifts[...]
    emit = strength[...] * (occupation[...] + 1.0)
    absorb = strength[...] * occupation[...]
    for kind, (high, low) in enumerate(((emit, absorb), (absorb, emit))):
        column = jnp.sum(jnp.where(up, high, 0.0) + jnp.where(down, low, 0.0), axis=1, keepdims=True)
        taps[kind] = jnp.broadcast_to(column, (PIECE, LANES))
    odd_row = (lax.broadcasted_iota(jnp.int32, (8, LANES), 0) & 1) == 1
    for kind in range(2):
        for d in range(2 * RING + 1):
            even_taps[kind, d] = spread(taps[kind, pl.ds(2 * d + 1, 1), :])
            odd_taps[kind, d] = jnp.where(
                odd_row, spread(taps[kind, pl.ds(2 * d + 2, 1), :]), spread(taps[kind, pl.ds(2 * d, 1), :])
            )

    loads[2].wait()
    for r in range(PAIRS):
        narrow_ret[r] = jnp.where(odd_row, spread(ret_in[1, pl.ds(r, 1), :]), spread(ret_in[0, pl.ds(r, 1), :]))
    for e in range(2):
        for v in range(PAIRS // 8):
            wide_ret[pl.ds(16 * v + e, 8, stride=2), :] = ret_in[e, rows8(8 * v), :]
    loads[3].wait()

    def widen(n, carry):
        for v in range(PAIRS // 8):
            value = links[n, rows8(8 * v), :]
            for e in range(2):
                wide_links[pl.ds(n * ROWS + 16 * v + e, 8, stride=2), :] = value
        return carry

    lax.fori_loop(0, NB, widen, 0)

    def widen_pair(h, carry):
        for v in range(PAIRS // 8):
            value = jnp.where(outer, links[2 * h, rows8(8 * v), :], half_turn(links[2 * h + 1, rows8(8 * v), :]))
            pair_links[h, rows8(8 * v), :] = value
            for e in range(2):
                wide_pairs[pl.ds(h * ROWS + 16 * v + e, 8, stride=2), :] = value
        return carry

    lax.fori_loop(0, NB // 2, mark_inner, 0)
    couple_own(greater_buf.at[0])
    couple_steps(0, NB)
    couple_inner(coupled.at[0])
    spread_forward(0, 0)
    lax.fori_loop(0, NB // 4, mark_outer, 0)
    lax.fori_loop(0, NB // 2, widen_pair, 0)

    def iteration(t, carry):
        edges_finish(1, t)
        couple_halo(coupled.at[t])
        spread_start(1, t)
        mix(0, t)
        spread_forward(1, t)
        collect(0, t)
        edges_start(0, arrived.at[0, t], t)
        couple_own(arrived.at[0, t])
        couple_steps(0, 4)
        mix(1, t)
        couple_steps(4, NB)
        couple_inner(sigma)
        edges_finish(0, t)
        couple_halo(sigma)
        dress(sigma, lesser_buf.at[0], lesser_buf.at[t + 1], narrow_ret, wide_ret)

        @pl.when(t < ITERS - 1)
        def _():
            spread_start(0, t + 1)

        collect(1, t)
        dress(arrived.at[1, t], greater_buf.at[0], greater_buf.at[t + 1], narrow_ret, wide_ret)

        @pl.when(t < ITERS - 1)
        def _():
            edges_start(1, greater_buf.at[t + 1], t + 1)
            couple_own(greater_buf.at[t + 1])
            couple_steps(0, NB)
            couple_inner(coupled.at[t + 1])
            spread_forward(0, t + 1)

        return carry

    lax.fori_loop(0, ITERS, iteration, 0)

    for e in range(2):
        for v in range(PAIRS // 8):
            out_lesser[e, rows8(8 * v), :] = lesser_buf[ITERS, pl.ds(16 * v + e, 8, stride=2), :]
            out_greater[e, rows8(8 * v), :] = greater_buf[ITERS, pl.ds(16 * v + e, 8, stride=2), :]

    def drain(t, carry):
        def pieces(m, inner):
            for kind in range(2):
                here = band.at[kind, t, piece(RING)]
                for side in range(2):
                    await_bytes(here, z_send.at[kind, t, side, m])
            return inner

        def sent(m, inner):
            for kind in range(2):
                await_bytes(band.at[kind, t, piece(RING)], a1_send.at[kind, t, m])
                await_bytes(mixed.at[kind, t, piece(0)], a2_send.at[kind, t, m])
            return inner

        lax.fori_loop(0, RING, pieces, 0)
        lax.fori_loop(0, RING - 1, sent, 0)
        for side in range(2):
            for kind in range(2):
                await_bytes(left_in.at[kind, t, whole], x_send.at[kind, t, side])
        return carry

    lax.fori_loop(0, ITERS, drain, 0)


def body(lesser, greater, retarded, coupling, offsets, shifts, strength, occupation):
    f32 = jnp.float32
    vmem = functools.partial(pl.BlockSpec, memory_space=pltpu.VMEM)
    outside = functools.partial(pl.BlockSpec, memory_space=pltpu.HBM)
    lanes = lesser.shape[-1]
    dma = pltpu.SemaphoreType.DMA
    return pl.pallas_call(
        kernel,
        out_shape=(jax.ShapeDtypeStruct(lesser.shape, f32),) * 2,
        in_specs=[outside()] * 8,
        out_specs=(vmem(), vmem()),
        scratch_shapes=[
            pltpu.VMEM(offsets.shape, jnp.int32),
            pltpu.VMEM((1, shifts.shape[0]), jnp.int32),
            pltpu.VMEM((1, shifts.shape[0]), f32),
            pltpu.VMEM((1, shifts.shape[0]), f32),
            pltpu.VMEM((2, 2, PAIRS, lanes), f32),
            pltpu.VMEM((2, PAIRS, lanes), f32),
            pltpu.VMEM((NB, PAIRS, lanes), f32),
            pltpu.VMEM((NB * ROWS, lanes), f32),
            pltpu.VMEM((PAIRS, 8, lanes), f32),
            pltpu.VMEM((ROWS, lanes), f32),
            pltpu.VMEM((2, PIECE, lanes), f32),
            pltpu.VMEM((2, 2 * RING + 1, 8, lanes), f32),
            pltpu.VMEM((2, 2 * RING + 1, 8, lanes), f32),
            pltpu.VMEM((ITERS + 1, PADDED, lanes), f32),
            pltpu.VMEM((ITERS + 1, PADDED, lanes), f32),
            pltpu.VMEM((ITERS, PADDED, lanes), f32),
            pltpu.VMEM((2, ITERS, PADDED, lanes), f32),
            pltpu.VMEM((2, ITERS, PADDED, lanes), f32),
            pltpu.VMEM((2, ITERS, 3 * PADDED, lanes), f32),
            pltpu.VMEM((2, ITERS, PADDED, lanes), f32),
            pltpu.VMEM((2, ITERS, PADDED, lanes), f32),
            pltpu.VMEM((NB // 2, PAIRS, lanes), f32),
            pltpu.VMEM((NB // 2 * ROWS, lanes), f32),
            pltpu.VMEM((NB // 2, 2 * lanes, 2 * lanes), jnp.bfloat16),
            pltpu.VMEM((NB // 4, 2 * lanes, 2 * lanes), jnp.bfloat16),
            pltpu.VMEM((ROWS, 2 * lanes), jnp.bfloat16),
            pltpu.VMEM((NB, ROWS // 8, 8, lanes), f32),
            pltpu.VMEM((ROWS, lanes), f32),
            pltpu.VMEM((PAIRS, 8, lanes), f32),
            pltpu.VMEM((ROWS, lanes), f32),
            dma((8,)),
            dma((2, ITERS, RING - 1)),
            dma((2, ITERS, RING)),
            dma((2, ITERS, 2, RING)),
            dma((2, ITERS, 2, RING)),
            dma((2, ITERS, RING - 1)),
            dma((2, ITERS, RING)),
            dma((2, ITERS, 2)),
            dma((2, ITERS, 2)),
        ],
        compiler_params=pltpu.CompilerParams(
            collective_id=0, has_side_effects=True, vmem_limit_bytes=63 * 1024 * 1024
        ),
    )(
        lesser, greater, retarded, coupling, offsets,
        shifts.reshape(1, -1), strength.reshape(1, -1), occupation.reshape(1, -1),
    )


def solution(mesh):
    placed = (
        P("energy", None, "slab"),
        P("energy", None, "slab"),
        P("energy", None, "slab"),
        P(None, None, "slab"),
        P(None, "slab"),
        P(),
        P(),
        P(),
    )
    return jax.shard_map(
        body,
        mesh=mesh,
        in_specs=placed,
        out_specs=(P("energy", None, "slab"), P("energy", None, "slab")),
        check_vma=False,
    )
```
